256 devices in a mesh: grp: 8 (over x, z_lo), dev: 32 (over y, z_hi, core).
Axes of the slice: x: 4, y: 4, z: 8 (z_hi: 4, z_lo: 2; z = z_hi * 2 + z_lo), core: 2. Of those that a mesh axis runs over, the one named last changes fastest.
Arguments:
- hidden_first: bfloat16 [65536, 8192], P(('grp', 'dev')), may hold values from -24 to 24
- logit_grads: bfloat16 [65536, 512], P(('grp', 'dev')), may hold values from -0.00018310547 to 0.00018310547
- hidden_second: bfloat16 [65536, 8192], P(('grp', 'dev')), may hold values from -400 to 400
- labels_second: int32 [65536], P(('grp', 'dev')), may hold values from 0 to 511
- master: float32 [8192, 512], P(('grp', 'dev')), may hold values from -0.0625 to 0.0625
- moment_one: float32 [8192, 512], P(('grp', 'dev')), may hold values from -0.00390625 to 0.00390625
- moment_two: float32 [8192, 512], P(('grp', 'dev')), may hold values from 1e-08 to 1e-06
Outputs:
- new_master: float32 [8192, 512], P(('grp', 'dev'))
- new_moment_one: float32 [8192, 512], P(('grp', 'dev'))
- new_moment_two: float32 [8192, 512], P(('grp', 'dev'))
- loss_second: float32 [65536], P(('grp', 'dev'))
The draws below stay inside these ranges and needn't reach their ends.
All inputs are finite; a program needn't handle non-finite values.
Results may differ from the reference program's by a relative error of at most 0.0014.
Values may be sent and summed in bfloat16 or wider, within the bound.
No kernel may reach another device: no remote copies, remote signals or barrier semaphores. Data moves between devices by JAX's collectives and lax.ppermute only.
A program may use at most 128 MiB of HBM per device.

```python
import math
import jax
import jax.numpy as jnp
from jax import lax

D = 8192
V = 512
STEP = 10
TOKENS = 65536


def draw_hidden_second(key, part):
    key = jax.random.fold_in(key, 7)
    first_key = jax.random.fold_in(key, 0)
    values = jnp.clip(jax.random.normal(first_key, (TOKENS, D), jnp.float32), -6.0, 6.0)
    return values.astype(jnp.bfloat16)


def with_ends(array, own_key, low, high):
    index_at = [jax.random.randint(jax.random.fold_in(own_key, axis), (), 0, length) for axis, length in enumerate(array.shape)]
    longest = array.shape.index(max(array.shape))
    next_to = index_at[:longest] + [(index_at[longest] + 1) % array.shape[longest]] + index_at[longest + 1:]
    return array.at[tuple(index_at)].set(low).at[tuple(next_to)].set(high)


def with_spikes(drawn, own_key, source, target, shards_of, factor):
    owner, partner = [(jnp.arange(drawn.shape[dim]) // (drawn.shape[dim] // shards_of)).reshape([-1 if axis == dim else 1 for axis in range(drawn.ndim)]) for dim in (source, target)]
    chosen = jax.random.permutation(own_key, shards_of)[partner]
    strong = (owner == chosen) | (owner == (partner + shards_of // 2) % shards_of)
    return jnp.where(strong, factor * drawn, drawn)


def shard_levels(own_key, shape, shards, least, largest):
    level, own = 1.0, jax.random.fold_in(own_key, 6)
    for position, shards_of in shards:
        heights = jnp.exp(jax.random.uniform(jax.random.fold_in(own, position), (shards_of,), jnp.float32, least / len(shards), largest / len(shards)))
        level = level * jnp.repeat(heights, shape[position] // shards_of).reshape([-1 if axis == position else 1 for axis in range(len(shape))])
    return level


def noise(own_key, shape, deviation, reach, cuts=(), kind=jnp.bfloat16):
    values = jax.random.normal(own_key, shape, jnp.float32) * deviation
    if len(cuts) > 0:
        values = shard_levels(own_key, shape, cuts, -0.22, 0.18) * values
    return jnp.clip(values, min=-reach, max=reach).astype(kind)


def heavy_noise(own_key, extent, deviation, most, pieces, heavy, held_as=jnp.bfloat16):
    drawn = deviation * jax.random.normal(own_key, extent, jnp.float32)
    if pieces:
        drawn = drawn * shard_levels(own_key, extent, pieces, -0.22, 0.18)
    return jnp.clip(with_spikes(drawn, jax.random.fold_in(own_key, 3), *heavy), -most, most).astype(held_as)


def setup_inputs(seed: int = 0) -> dict:
    splits = jax.random.split(jax.random.key(seed), 8)
    return {
        "hidden_first": heavy_noise(splits[0], (TOKENS, D), 1.0, 24.0, ((0, 256),), (0, 1, 256, 6.0)),
        "logit_grads": noise(splits[1], (TOKENS, V), (0.003 / TOKENS ** 0.5), 0.00018310547, ((0, 256),)),
        "hidden_second": draw_hidden_second(jax.random.fold_in(splits[7], 71), 0),
        "labels_second": with_ends(jax.random.randint(splits[3], (TOKENS,), 0, V), jax.random.fold_in(splits[3], 1), 0, V - 1).astype(jnp.int32),
        "master": noise(splits[4], (D, V), D ** -0.5, 0.0625, ((0, 256),), jnp.float32),
        "moment_one": noise(splits[5], (D, V), 0.0003, 0.00390625, ((0, 256),), jnp.float32),
        "moment_two": jnp.clip(jnp.exp(math.log(9.999999974752427e-07) - 4.6051702 * jax.random.uniform(splits[6], (D, V), jnp.float32) ** shard_levels(splits[6], (D, V), ((0, 256),), -0.2, 0.2)), 9.99999993922529e-09, 9.999999974752427e-07),
    }


def reference(hidden_first, logit_grads, hidden_second, labels_second, master, moment_one, moment_two):
    weight_grad = jnp.dot(hidden_first.T, logit_grads, preferred_element_type=jnp.float32)
    new_moment_one = 0.9 * moment_one + 0.1 * weight_grad
    new_moment_two = 0.95 * moment_two + 0.05 * weight_grad * weight_grad
    first_fix = 1.0 - 0.9 ** STEP
    second_fix = 1.0 - 0.95 ** STEP
    update = new_moment_one / first_fix / (jnp.sqrt(new_moment_two / second_fix) + 1e-08) + 0.1 * master
    new_master = master - 0.002 * update
    new_copy = new_master.astype(jnp.bfloat16)
    logits = jnp.dot(hidden_second, new_copy, preferred_element_type=jnp.float32)
    top = lax.optimization_barrier(jnp.max(logits, axis=1, keepdims=True))
    lse = top + jnp.log(lax.optimization_barrier(jnp.sum(jnp.exp(logits - top), axis=1, keepdims=True)))
    onehot = (labels_second[:, None] == jnp.arange(logits.shape[1], dtype=jnp.int32)[None, :]).astype(jnp.float32)
    loss_second = lse[:, 0] - lax.optimization_barrier(jnp.sum(onehot * logits, axis=1))
    return (new_master, new_moment_one, new_moment_two, loss_second)
```

```python
import jax
import jax.numpy as jnp
from jax import lax
from jax.experimental import pallas as pl
from jax.experimental.pallas import tpu as pltpu
from jax.sharding import Mesh
from jax.sharding import PartitionSpec as P

STEP = 10
AXES = ("x", "zl", "y", "zh", "c")
SIZES = (4, 2, 4, 4, 2)
F32, BF16, I16, I32 = jnp.float32, jnp.bfloat16, jnp.int16, jnp.int32
T = 128
PARAMS = pltpu.CompilerParams(vmem_limit_bytes=52 * 1024 * 1024)


def encode(tile):
    most = jnp.max(jnp.abs(tile), axis=0, keepdims=True)
    level = jnp.floor(8.0 * (14.98 - jnp.log2(jnp.maximum(most, 1e-30))))
    scale = jnp.exp2(level * 0.125)
    return jnp.round(tile * scale).astype(I32).astype(I16), level


def rows(i, n=T):
    return slice(i * n, (i + 1) * n)


def levels_tile(levels):
    short = 16 - len(levels)
    if short:
        levels = levels + [jnp.zeros((short, T), F32)]
    return jnp.concatenate(levels, axis=0).astype(I32).astype(I16)


def scales_of(ref, first):
    level = ref[first : first + 16, :].astype(I32).astype(F32)
    return jnp.exp2(level * -0.125)


def decode(ref, i, inverse):
    return ref[rows(i), :].astype(I32).astype(F32) * inverse[i : i + 1, :]


def grad_kernel(place, h, hr, l, lr, x0, x1, x2, x3, y0, y1, y2, y3, lt, prod, ylevels):
    k = pl.program_id(0)
    y = place[1]

    @pl.when(k == 0)
    def _():
        lt[:, 0:256] = l[...].T
        lt[:, 256:512] = lr[...].T

    prod[...] = jnp.dot(lt[:, 0:256], h[...], preferred_element_type=F32) + jnp.dot(
        lt[:, 256:512], hr[...], preferred_element_type=F32
    )

    def lanes(zl, j, half):
        at = zl * 1024 + lax.rem(y + j, 4) * 256 + half * T
        return pl.ds(pl.multiple_of(at, T), T)

    for step, out in enumerate((x0, x1, x2, x3)):

        @pl.when(k == step)
        def _(step=step, out=out):
            levels = []
            for zl in range(2):
                for j in range(4):
                    for half in range(2):
                        tile = prod[0:T, lanes(zl, j, half)]
                        i = zl * 8 + j * 2 + half
                        if step == 0:
                            out[rows(i), :] = tile
                        else:
                            out[rows(i), :], level = encode(tile)
                            levels.append(level)
            if step:
                out[2048:2064, :] = levels_tile(levels)

    for j, out in enumerate((y0, y1, y2, y3)):
        for zl in range(2):
            for half in range(2):
                tile = prod[T : 2 * T, lanes(zl, j, half)]
                i = k * 4 + zl * 2 + half
                at = pl.ds(pl.multiple_of(i * T, T), T)
                if j == 0:
                    out[at, :] = tile
                else:
                    out[at, :], level = encode(tile)
                    ylevels[j - 1, pl.ds(i, 1), :] = level

    @pl.when(k == 3)
    def _():
        for j, out in enumerate((y1, y2, y3)):
            out[2048:2064, :] = ylevels[j].astype(I32).astype(I16)


def first_sum_kernel(x0, x1, x2, x3, y0, y1, y2, y3, xs0, xs1, xs2, xs3, ys0, ys1, ys2, ys3):
    for own, taken, outs, index in (
        (x0, (x1, x2, x3), (xs0, xs1, xs2, xs3), lambda d, zl, half: zl * 8 + d * 2 + half),
        (y0, (y1, y2, y3), (ys0, ys1, ys2, ys3), lambda d, zl, half: d * 4 + zl * 2 + half),
    ):
        inverse = [scales_of(r, 2048) for r in taken]
        for d, out in enumerate(outs):
            levels = []
            for zl in range(2):
                for half in range(2):
                    i = index(d, zl, half)
                    total = own[rows(i), :]
                    for r, s in zip(taken, inverse):
                        total += decode(r, i, s)
                    o = zl * 2 + half
                    if d == 0:
                        out[rows(o), :] = total
                    else:
                        out[rows(o), :], level = encode(total)
                        levels.append(level)
            if d:
                out[512:528, :] = levels_tile(levels)


def second_sum_kernel(x0, x1, x2, x3, y0, y1, y2, y3, out):
    sx = [scales_of(r, 512) for r in (x1, x2, x3)]
    sy = [scales_of(r, 512) for r in (y1, y2, y3)]
    low = lax.broadcasted_iota(I32, (T, T), 1) < 64
    for zl in range(2):
        for half in range(2):
            i = zl * 2 + half
            a, b = x0[rows(i), :], y0[rows(i), :]
            for r, s in zip((x1, x2, x3), sx):
                a += decode(r, i, s)
            for r, s in zip((y1, y2, y3), sy):
                b += decode(r, i, s)
            first = jnp.where(low, a, pltpu.roll(b, 64, 1))
            second = jnp.where(low, pltpu.roll(a, 64, 1), b)
            for n, tile in ((0, first), (1, second)):
                at = (zl * 4 + half * 2 + n) * 144
                out[at : at + T, :], level = encode(tile)
                out[at + T : at + 144, :] = levels_tile([level])


def third_sum_kernel(taken, out):
    total = None
    for n in range(8):
        at = n * 144
        inverse = scales_of(taken, at + T)[0:1, :]
        part = taken[at : at + T, :].astype(I32).astype(F32) * inverse
        total = part if total is None else total + part
    out[...] = total.T


def adam_kernel(place, own, other, master, one, two, new_master, new_one, new_two, copy):
    c = place[2]
    first = pl.ds(pl.multiple_of(c * 32, 32), 32)
    second = pl.ds(pl.multiple_of(64 + c * 32, 32), 32)
    mine = jnp.concatenate([own[first, :], own[second, :]], axis=1)
    theirs = jnp.concatenate([other[first, :], other[second, :]], axis=1)
    grad = jnp.where(
        c == 0,
        jnp.concatenate([mine, theirs], axis=1),
        jnp.concatenate([theirs, mine], axis=1),
    )
    moment_one = 0.9 * one[...] + 0.1 * grad
    moment_two = 0.95 * two[...] + 0.05 * grad * grad
    first_fix = 1.0 - 0.9**STEP
    second_fix = 1.0 - 0.95**STEP
    update = (
        moment_one / first_fix / (jnp.sqrt(moment_two / second_fix) + 1e-08) + 0.1 * master[...]
    )
    weights = master[...] - 0.002 * update
    new_master[...] = weights
    new_one[...] = moment_one
    new_two[...] = moment_two
    copy[...] = weights.astype(BF16)


def spread_kernel(place, own, other, out):
    c = place[2]
    low = pl.ds(pl.multiple_of(c * 256, 256), T)
    high = pl.ds(pl.multiple_of(c * 256 + T, T), T)
    parts = []
    for lanes in (low, high):
        mine, theirs = own[:, lanes], other[:, lanes]
        parts.append(jnp.where(c == 0, mine, theirs))
        parts.append(jnp.where(c == 0, theirs, mine))
    block = jnp.concatenate(parts, axis=0)
    for n in range(8):
        out[rows(n), :] = block


def head_kernel(
    place, h, hr, labels, labels_r, x0, x1, x2, x3, y0, y1, y2, y3, stats, stats_r, logits
):
    k = pl.program_id(0)
    y, c = place[1], place[2]

    for step, wx in enumerate((x0, x1, x2, x3)):

        @pl.when(k == step)
        def _(step=step, wx=wx):
            for n, tokens in enumerate((h, hr)):
                total = None
                for s, wy in enumerate((y0, y1, y2, y3)):
                    for zl in range(2):
                        at = zl * 1024 + lax.rem(y - s + 4, 4) * 256
                        left = tokens[:, pl.ds(pl.multiple_of(at, 256), 256)]
                        a = s * 512 + zl * 256
                        b = step * 512 + zl * 256
                        right = jnp.concatenate([wx[a : a + 256, :], wy[b : b + 256, :]], axis=1)
                        term = jnp.dot(left, right, preferred_element_type=F32)
                        total = term if total is None else total + term
                if step == 0:
                    logits[n] = total
                else:
                    logits[n] += total

    @pl.when(k == 3)
    def _():
        lane = lax.broadcasted_iota(I32, (256, T), 1)
        column = lax.broadcasted_iota(I32, (256, 256), 1) + c * 256
        for n, (label, out) in enumerate(((labels, stats), (labels_r, stats_r))):
            rows_ = logits[n]
            top = jnp.max(rows_, axis=1, keepdims=True)
            total = jnp.sum(jnp.exp(rows_ - top), axis=1, keepdims=True)
            hit = jnp.sum(jnp.where(column == label[...], rows_, 0.0), axis=1, keepdims=True)
            out[...] = jnp.where(lane == 0, top, jnp.where(lane == 1, total, hit))


def loss_kernel(a, b, out):
    top = jnp.maximum(a[:, 0:1], b[:, 0:1])
    total = a[:, 1:2] * jnp.exp(a[:, 0:1] - top) + b[:, 1:2] * jnp.exp(b[:, 0:1] - top)
    loss = top + jnp.log(total) - (a[:, 2:3] + b[:, 2:3])
    out[...] = jnp.broadcast_to(loss, (256, T)).T[0:1, :]


def shape(*dims, dtype=F32):
    return jax.ShapeDtypeStruct(dims, dtype)


def whole(*dims):
    return pl.BlockSpec(dims, lambda *_: (0,) * len(dims))


def simple(kernel, outs, *args, place=None):
    specs = [whole(*a.shape) for a in args]
    many = isinstance(outs, (list, tuple))
    out_specs = [whole(*o.shape) for o in outs] if many else whole(*outs.shape)
    return pl.pallas_call(
        kernel,
        out_shape=outs,
        grid_spec=pltpu.PrefetchScalarGridSpec(
            num_scalar_prefetch=0 if place is None else 1,
            grid=(1,),
            in_specs=specs,
            out_specs=out_specs,
        ),
        compiler_params=PARAMS,
    )(*(() if place is None else (place,)), *args)


def swap(a):
    return lax.ppermute(a, "c", [(0, 1), (1, 0)])


def shift(a, axis, by):
    return lax.ppermute(a, axis, [(i, (i + by) % 4) for i in range(4)])


def on_device(
    hidden_first, logit_grads, hidden_second, labels_second, master, moment_one, moment_two
):
    place = jnp.stack([lax.axis_index("x"), lax.axis_index("y"), lax.axis_index("c")])
    labels = labels_second[:, None]

    other_grads = swap(logit_grads)
    other_first = swap(hidden_first)
    hold = lax.optimization_barrier((other_first, hidden_second, labels))
    other_first = hold[0]
    other_second = swap(hold[1])
    other_labels = swap(hold[2])

    near = pl.BlockSpec((256, 2048), lambda k, p: (0, lax.rem(p[0] + k, 4)))
    half = pl.BlockSpec((256, 256), lambda k, p: (0, p[2]))
    message = shape(2064, T, dtype=I16)
    sums = pl.pallas_call(
        grad_kernel,
        out_shape=[shape(2048, T), message, message, message] * 2,
        grid_spec=pltpu.PrefetchScalarGridSpec(
            num_scalar_prefetch=1,
            grid=(4,),
            in_specs=[near, near, half, half],
            out_specs=[whole(2048, T), whole(2064, T), whole(2064, T), whole(2064, T)] * 2,
            scratch_shapes=[
                pltpu.VMEM((256, 512), BF16),
                pltpu.VMEM((256, 2048), F32),
                pltpu.VMEM((3, 16, T), F32),
            ],
        ),
        compiler_params=PARAMS,
    )(place, hidden_first, other_first, logit_grads, other_grads)

    def cross(blocks, first, second):
        sent = [None] * 8
        for by in (2, 1, 3):
            sent[by] = shift(blocks[by], first, by)
            sent[4 + by] = shift(blocks[4 + by], second, by)
        sent[0], sent[4] = blocks[0], blocks[4]
        return sent

    message = shape(528, T, dtype=I16)
    sums = simple(
        first_sum_kernel,
        [shape(512, T), message, message, message] * 2,
        *cross(sums, "x", "y"),
    )
    chunks = simple(second_sum_kernel, shape(1152, T, dtype=I16), *cross(sums, "y", "x"))
    chunks = lax.all_to_all(chunks, ("zl", "zh"), 0, 0, tiled=True)
    total = simple(third_sum_kernel, shape(T, T), chunks)
    new_master, new_one, new_two, copy = simple(
        adam_kernel,
        [shape(32, 512)] * 3 + [shape(32, 512, dtype=BF16)],
        total,
        swap(total),
        master,
        moment_one,
        moment_two,
        place=place,
    )

    blocks = simple(spread_kernel, shape(1024, T, dtype=BF16), copy, swap(copy), place=place)
    blocks = lax.all_to_all(blocks, ("zl", "zh"), 0, 0, tiled=True).reshape(8, 2, 64, T)
    low, high = (blocks[:, n].reshape(512, T) for n in range(2))
    pieces = cross([low] * 4 + [high] * 4, "y", "x")
    low, high = jnp.concatenate(pieces[:4]), jnp.concatenate(pieces[4:])
    pieces = cross([low] * 4 + [high] * 4, "x", "y")

    back = pl.BlockSpec((256, 2048), lambda k, p: (0, lax.rem(p[0] - k + 4, 4)))
    stats, other_stats = pl.pallas_call(
        head_kernel,
        out_shape=[shape(256, T)] * 2,
        grid_spec=pltpu.PrefetchScalarGridSpec(
            num_scalar_prefetch=1,
            grid=(4,),
            in_specs=[back, back, whole(256, 1), whole(256, 1)] + [whole(2048, T)] * 8,
            out_specs=[whole(256, T)] * 2,
            scratch_shapes=[pltpu.VMEM((2, 256, 256), F32)],
        ),
        compiler_params=PARAMS,
    )(place, hidden_second, other_second, labels, other_labels, *pieces)
    loss = simple(loss_kernel, shape(1, 256), stats, swap(other_stats))
    return new_master, new_one, new_two, loss.reshape(256)


def solution(mesh):
    fine = Mesh(mesh.devices.reshape(SIZES), AXES)
    two, one = P(AXES, None), P(AXES)
    return jax.shard_map(
        on_device,
        mesh=fine,
        in_specs=(two, two, two, one, two, two, two),
        out_specs=(two, two, two, one),
        check_vma=False,
    )
```

```python
import jax
import jax.numpy as jnp
from jax import lax
from jax.experimental import pallas as pl
from jax.experimental.pallas import tpu as pltpu
from jax.sharding import Mesh
from jax.sharding import PartitionSpec as P

STEP = 10
AXES = ("x", "zl", "y", "zh", "c")
SIZES = (4, 2, 4, 4, 2)
F32, BF16, I16, I32 = jnp.float32, jnp.bfloat16, jnp.int16, jnp.int32
T = 128
ROUND = 12582912.0
ORDER = (2, 1, 3)


def encode(tiles):
    most = [jnp.max(jnp.abs(tile), axis=0, keepdims=True) for tile in tiles]
    most = jnp.concatenate(most, axis=0)
    level = jnp.floor(8.0 * (14.98 - jnp.log2(jnp.maximum(most, 1e-30))))
    scale = jnp.exp2(level * 0.125)
    whole_numbers = [
        ((tile * scale[i : i + 1, :] + ROUND) - ROUND).astype(I32).astype(I16)
        for i, tile in enumerate(tiles)
    ]
    return whole_numbers, level


def rows(i, n=T):
    return slice(i * n, (i + 1) * n)


def levels_tile(level):
    level = jnp.concatenate([level, jnp.zeros((16 - level.shape[0], T), F32)], axis=0)
    return level.astype(I32).astype(I16)


def scales_of(ref, first):
    level = ref[first : first + 16, :].astype(I32).astype(F32)
    return jnp.exp2(level * -0.125)


def added(refs, i, block=0):
    total = None
    for ref in refs:
        part = ref[block + i * 256 : block + i * 256 + 256, :].astype(I32).astype(F32)
        part *= scales_of(ref, block + 1024)[i : i + 1, :]
        total = part if total is None else total + part
    return total


def turn_kernel(place, l, lr, out):
    out[:, 0:256] = l[...].T
    out[:, 256:512] = lr[...].T


def pick_kernel(place, *refs):
    for i, h in enumerate(refs[:8]):
        refs[8][:, rows(i, 256)] = h[...]


def store(outs, tiles):
    tiles, level = encode(tiles)
    blocks = len(tiles) // 4
    for a in range(blocks):
        out, at = outs[a * len(outs) // blocks], a % (blocks // len(outs)) * 1040
        for i in range(4):
            out[at + i * 256 : at + i * 256 + 256, :] = tiles[a * 4 + i]
        out[at + 1024 : at + 1040, :] = levels_tile(level[rows(a, 4), :])


def grad_kernel(place, lt, *refs):
    hr, outs, tiles = refs[8], refs[9:], []
    for i, h in enumerate(refs[:8]):
        prod = jnp.dot(lt[:, 0:256], h[...], preferred_element_type=F32)
        prod += jnp.dot(lt[:, 256:512], hr[:, rows(i, 256)], preferred_element_type=F32)
        tiles += [prod[:, 0:T], prod[:, T:256]]
    store(outs, tiles)


def sum_kernel(place, *refs):
    taken, out = refs[:-1], refs[-1]
    tiles = []
    for a in range(out.shape[0] // 1040):
        tiles += [added(taken, i, a * 1040) for i in range(4)]
    store([out], tiles)


def second_sum_kernel(m0, m1, m2, m3, out):
    low = lax.broadcasted_iota(I32, (T, T), 1) < 64
    tiles = []
    for i in range(4):
        total = added((m0, m1, m2, m3), i)
        a, b = total[0:T, :], total[T:256, :]
        tiles.append(jnp.where(low, a, pltpu.roll(b, 64, 1)))
        tiles.append(jnp.where(low, pltpu.roll(a, 64, 1), b))
    tiles, level = encode(tiles)
    for i in range(8):
        out[i * 144 : i * 144 + T, :] = tiles[i]
        out[i * 144 + T : i * 144 + 144, :] = levels_tile(level[i : i + 1, :])


def owner_kernel(place, taken, master, one, two, given, kept, sent, out):
    c = place[2]
    total = None
    for n in range(8):
        at = n * 144
        inverse = scales_of(taken, at + T)[0:1, :]
        part = taken[at : at + T, :].astype(I32).astype(F32) * inverse
        total = part if total is None else total + part
    total = total.T
    lanes = pl.ds(pl.multiple_of(c * 256, 256), 256)
    mine = [r[:, lanes] for r in (master, one, two)]
    theirs = [given[rows(n, 32), :] for n in range(3)]
    results, copies = [], []
    for block in range(2):
        grad = jnp.concatenate(
            [total[block * 32 : block * 32 + 32], total[64 + block * 32 : 96 + block * 32]], axis=1
        )
        old, moment_one, moment_two = (
            jnp.where(c == block, a, b) for a, b in zip(mine, theirs)
        )
        moment_one = 0.9 * moment_one + 0.1 * grad
        moment_two = 0.95 * moment_two + 0.05 * grad * grad
        first_fix = 1.0 - 0.9**STEP
        second_fix = 1.0 - 0.95**STEP
        update = (
            moment_one / first_fix / (jnp.sqrt(moment_two / second_fix) + 1e-08) + 0.1 * old
        )
        weights = old - 0.002 * update
        results.append((weights, moment_one, moment_two))
        copies.append(weights.astype(BF16))
    for n in range(3):
        kept[rows(n, 32), :] = jnp.where(c == 0, results[0][n], results[1][n])
        sent[rows(n, 32), :] = jnp.where(c == 0, results[1][n], results[0][n])
    block = jnp.concatenate(
        [copies[0][:, 0:T], copies[1][:, 0:T], copies[0][:, T:], copies[1][:, T:]], axis=0
    )
    for n in range(8):
        out[rows(n), :] = block


def join_kernel(place, kept, given, *outs):
    first = place[2] == 0
    for n, out in enumerate(outs):
        a, b = kept[rows(n, 32), :], given[rows(n, 32), :]
        out[:, 0:256] = jnp.where(first, a, b)
        out[:, 256:512] = jnp.where(first, b, a)


def products(halves, tokens):
    totals = [None, None]
    for i in range(8):
        parts = [
            jnp.concatenate(
                [halves[i // 4][rows((i % 4 * 4 + zh) * 2 + p, 64), :] for zh in range(4)], axis=0
            )
            for p in range(2)
        ]
        weight = jnp.concatenate(parts, axis=1)
        for n in range(2):
            part = jnp.dot(tokens(n, i), weight, preferred_element_type=F32)
            totals[n] = part if i == 0 else totals[n] + part
    return totals


def first_head_kernel(place, w0, w1, *refs):
    total = refs[16]
    for n, term in enumerate(products((w0, w1), lambda n, i: refs[n * 8 + i][...])):
        total[rows(n, 256), :] = term


def next_head_kernel(place, w0, w1, *refs):
    before, total = refs[16:]
    for n, term in enumerate(products((w0, w1), lambda n, i: refs[n * 8 + i][...])):
        total[rows(n, 256), :] = before[rows(n, 256), :] + term


def last_head_kernel(place, w0, w1, *refs):
    before, labels, labels_r, stats, stats_r = refs[2:]
    totals = products((w0, w1), lambda n, i: refs[n][:, rows(i, 256)])
    lane = lax.broadcasted_iota(I32, (256, T), 1)
    column = lax.broadcasted_iota(I32, (256, 256), 1) + place[2] * 256
    for n, (label, out) in enumerate(((labels, stats), (labels_r, stats_r))):
        logits = before[rows(n, 256), :] + totals[n]
        top = jnp.max(logits, axis=1, keepdims=True)
        expsum = jnp.sum(jnp.exp(logits - top), axis=1, keepdims=True)
        hit = jnp.sum(jnp.where(column == label[...], logits, 0.0), axis=1, keepdims=True)
        out[...] = jnp.where(lane == 0, top, jnp.where(lane == 1, expsum, hit))


def loss_kernel(place, a, b, out):
    a, b = a[...].T, b[...].T
    top = jnp.maximum(a[0:1, :], b[0:1, :])
    total = a[1:2, :] * jnp.exp(a[0:1, :] - top) + b[1:2, :] * jnp.exp(b[0:1, :] - top)
    out[...] = top + jnp.log(total) - (a[2:3, :] + b[2:3, :])


def shape(*dims, dtype=F32):
    return jax.ShapeDtypeStruct(dims, dtype)


def whole(*dims):
    return pl.BlockSpec(dims, lambda *_: (0,) * len(dims))


def call(kernel, outs, place, args, specs=None):
    many = isinstance(outs, (list, tuple))
    specs = specs or [None] * len(args)
    specs = [s or whole(*a.shape) for s, a in zip(specs, args)]
    return pl.pallas_call(
        kernel,
        out_shape=outs,
        grid_spec=pltpu.PrefetchScalarGridSpec(
            num_scalar_prefetch=1,
            grid=(1,),
            in_specs=specs,
            out_specs=[whole(*o.shape) for o in outs] if many else whole(*outs.shape),
        ),
        compiler_params=pltpu.CompilerParams(vmem_limit_bytes=16 * 1024 * 1024),
        cost_estimate=pl.CostEstimate(flops=1, bytes_accessed=1, transcendentals=0),
    )(place, *args)


def columns(far, sign, other=False):
    def index(near, zl, place):
        x, y, c = place[0], place[1], place[2]
        c = 1 - c if other else c
        x = x + 8 + sign * (far * (1 - c) + near * c)
        y = y + 8 + sign * (far * c + near * (1 - c))
        return 0, lax.rem(x, 4) * 8 + zl * 4 + lax.rem(y, 4)

    return [
        pl.BlockSpec((256, 256), lambda _, p, near=near, zl=zl: index(near, zl, p))
        for near in range(4)
        for zl in range(2)
    ]


def swap(a):
    return lax.ppermute(a, "c", [(0, 1), (1, 0)])


def send(a, by, first):
    pairs = []
    for i in range(256):
        x, y, c = i // 64, i // 8 % 4, i % 2
        to = (x + by) % 4, (y + by) % 4
        pairs.append((i, i + ((to[0] - x) * 64 if (c == 0) == first else (to[1] - y) * 8)))
    return lax.ppermute(a, AXES, pairs)


def on_device(
    hidden_first, logit_grads, hidden_second, labels_second, master, moment_one, moment_two
):
    hold = lax.optimization_barrier
    place = jnp.stack([lax.axis_index("x"), lax.axis_index("y"), lax.axis_index("c")])
    labels = labels_second[:, None]
    states = (master, moment_one, moment_two)
    far_half = (1 - place[2]) * 256
    state = jnp.concatenate([lax.dynamic_slice(a, (0, far_half), (32, 256)) for a in states])

    other_grads = swap(logit_grads)
    def pick(far, after):
        h, after = hold((hidden_first, after))
        args = [h] * 8
        block = shape(256, 2048, dtype=BF16)
        return call(pick_kernel, block, place, args, columns(far, 1, True)), after

    def grad(far, taken):
        return call(
            grad_kernel,
            [shape(2080, T, dtype=I16)] * 2,
            place,
            (turned, *[hidden_first] * 8, taken),
            [None] + columns(far, 1) + [None],
        )

    block, _ = pick(ORDER[0], place)
    block, other_grads = hold((block, other_grads))
    taken = swap(block)
    half = pl.BlockSpec((256, 256), lambda step, p: (0, p[2]))
    turned = call(
        turn_kernel,
        shape(256, 512, dtype=BF16),
        place,
        (logit_grads, other_grads),
        [half, half],
    )
    block, turned = pick(ORDER[1], turned)
    following = swap(block)
    two = grad(2, taken)
    block, two = pick(3, two)
    taken, following = following, swap(block)
    turned, block = hold((turned, block))
    relayed = send(two[0], 1, True), send(two[1], 3, True)
    ahead = grad(1, taken)
    block, ahead = pick(0, ahead)
    taken, following = following, swap(block)
    turned, block = hold((turned, block))
    from_behind = [None, send(ahead[1], 1, True)]
    back = grad(3, taken)
    from_ahead = [send(back[0], 3, True), None]
    half_message = shape(2080, T, dtype=I16)
    from_behind[0] = send(call(sum_kernel, half_message, place, (ahead[0], relayed[0])), 1, True)
    from_ahead[1] = send(call(sum_kernel, half_message, place, (back[1], relayed[1])), 3, True)
    own = grad(0, following)
    sums = [own, from_behind, from_ahead]
    sums, state = hold((sums, state))
    state = swap(state)

    blocks = [None] * 4
    for far in ORDER + (0,):
        spec = pl.BlockSpec((1040, T), lambda s, p, far=far: (far % 2, 0))
        blocks[far] = call(
            sum_kernel,
            shape(1040, T, dtype=I16),
            place,
            [taken[far // 2] for taken in sums],
            [spec] * 3,
        )
        if far:
            blocks[far] = send(blocks[far], far, False)
    blocks, second, labels = hold((blocks, hidden_second, labels))
    other_second, other_labels = swap(second), swap(labels)
    chunks = call(
        lambda _, *refs: second_sum_kernel(*refs), shape(1152, T, dtype=I16), place, blocks
    )
    chunks = lax.all_to_all(chunks, ("zl", "zh"), 0, 0, tiled=True)
    kept, sent, copies = call(
        owner_kernel,
        [shape(96, 256)] * 2 + [shape(1024, T, dtype=BF16)],
        place,
        (chunks, *states, state),
    )

    copies = lax.all_to_all(copies, ("zl", "zh"), 0, 0, tiled=True)
    pieces = [copies] + [None] * 3
    for far in ORDER:
        pieces[far] = send(copies, far, False)
    picked = [
        call(pick_kernel, shape(256, 2048, dtype=BF16), place, [h] * 8, columns(2, -1))
        for h in (hidden_second, other_second)
    ]
    pieces, picked, other_labels = hold((pieces, picked, other_labels))
    own = jnp.concatenate(pieces[:2]), jnp.concatenate(pieces[2:])
    behind, ahead = [None, None], [None, None]
    behind[0], ahead[1] = send(own[0], 1, True), send(own[1], 3, True)
    behind[1], ahead[0] = send(own[1], 1, True), send(own[0], 3, True)
    tokens = [hidden_second] * 8 + [other_second] * 8
    specs = [[None] * 2 + columns(far, -1) * 2 for far in range(4)]
    total = call(first_head_kernel, shape(512, 256), place, (*own, *tokens), specs[0])
    behind[0], ahead[1], total = hold((behind[0], ahead[1], total))
    two = send(behind[0], 1, True), send(ahead[1], 3, True)
    behind, sent = hold((behind, sent))
    sent = swap(sent)
    for far, piece in ((1, behind), (3, ahead)):
        total = call(
            next_head_kernel,
            shape(512, 256),
            place,
            (*piece, *tokens, total),
            specs[far] + [None],
        )
    two, total = hold((two, total))
    stats, other_stats = call(
        last_head_kernel,
        [shape(256, T)] * 2,
        place,
        (*two, *picked, total, labels, other_labels),
    )
    updated = call(join_kernel, [shape(32, 512)] * 3, place, (kept, sent))
    other_stats, updated = hold((swap(other_stats), updated))
    loss = call(loss_kernel, shape(1, 256), place, (stats, other_stats))
    return *updated, loss.reshape(256)


def solution(mesh):
    fine = Mesh(mesh.devices.reshape(SIZES), AXES)
    two, one = P(AXES, None), P(AXES)
    return jax.shard_map(
        on_device,
        mesh=fine,
        in_specs=(two, two, two, one, two, two, two),
        out_specs=(two, two, two, one),
        check_vma=False,
    )
```

```python
import jax
import jax.numpy as jnp
from jax import lax
from jax.experimental import pallas as pl
from jax.experimental.pallas import tpu as pltpu
from jax.sharding import Mesh
from jax.sharding import PartitionSpec as P

STEP = 10
AXES = ("x", "zl", "y", "zh", "c")
SIZES = (4, 2, 4, 4, 2)
F32, BF16, I16, I32 = jnp.float32, jnp.bfloat16, jnp.int16, jnp.int32
T = 128
ROUND = 12582912.0
ORDER = (2, 1, 3)


def encode(tiles):
    most = [jnp.max(jnp.abs(tile), axis=0, keepdims=True) for tile in tiles]
    most = jnp.concatenate(most, axis=0)
    level = jnp.floor(8.0 * (14.98 - jnp.log2(jnp.maximum(most, 1e-30))))
    scale = jnp.exp2(level * 0.125)
    whole_numbers = [
        ((tile * scale[i : i + 1, :] + ROUND) - ROUND).astype(I32).astype(I16)
        for i, tile in enumerate(tiles)
    ]
    return whole_numbers, level


def rows(i, n=T):
    return slice(i * n, (i + 1) * n)


def levels_tile(level):
    level = jnp.concatenate([level, jnp.zeros((16 - level.shape[0], T), F32)], axis=0)
    return level.astype(I32).astype(I16)


def scales_of(ref, first):
    level = ref[first : first + 16, :].astype(I32).astype(F32)
    return jnp.exp2(level * -0.125)


def added(refs, i, block=0):
    total = None
    for ref in refs:
        part = ref[block + i * 256 : block + i * 256 + 256, :].astype(I32).astype(F32)
        part *= scales_of(ref, block + 1024)[i : i + 1, :]
        total = part if total is None else total + part
    return total


def turn_kernel(place, l, lr, out):
    out[:, 0:256] = l[...].T
    out[:, 256:512] = lr[...].T


def pick_kernel(place, *refs):
    for i, h in enumerate(refs[:8]):
        refs[8][:, rows(i, 256)] = h[...]


def store(out, tiles):
    tiles, level = encode(tiles)
    for a in range(len(tiles) // 4):
        at = a * 1040
        for i in range(4):
            out[at + i * 256 : at + i * 256 + 256, :] = tiles[a * 4 + i]
        out[at + 1024 : at + 1040, :] = levels_tile(level[rows(a, 4), :])


def grad_kernel(place, lt, *refs):
    hr, relayed, out, tiles = refs[4], refs[5:-1], refs[-1], []
    for i, h in enumerate(refs[:4]):
        prod = jnp.dot(lt[:, 0:256], h[...], preferred_element_type=F32)
        prod += jnp.dot(lt[:, 256:512], hr[:, rows(i, 256)], preferred_element_type=F32)
        for half in range(2):
            tile = prod[:, rows(half)]
            if relayed:
                tile += added(relayed, i % 2 * 2 + half, i // 2 * 1040)
            tiles.append(tile)
    store(out, tiles)


def sum_kernel(place, *refs):
    store(refs[-1], [added(refs[:-1], i) for i in range(4)])


def second_sum_kernel(place, m0, m1, m2, m3, out):
    low = lax.broadcasted_iota(I32, (T, T), 1) < 64
    tiles = []
    for i in range(4):
        total = added((m0, m1, m2, m3), i)
        a, b = total[0:T, :], total[T:256, :]
        tiles.append(jnp.where(low, a, pltpu.roll(b, 64, 1)))
        tiles.append(jnp.where(low, pltpu.roll(a, 64, 1), b))
    tiles, level = encode(tiles)
    for i in range(8):
        out[i * 144 : i * 144 + T, :] = tiles[i]
        out[i * 144 + T : i * 144 + 144, :] = levels_tile(level[i : i + 1, :])


def owner_kernel(place, taken, master, one, two, given, kept, sent, out):
    c = place[2]
    total = None
    for n in range(8):
        at = n * 144
        inverse = scales_of(taken, at + T)[0:1, :]
        part = taken[at : at + T, :].astype(I32).astype(F32) * inverse
        total = part if total is None else total + part
    total = total.T
    lanes = pl.ds(pl.multiple_of(c * 256, 256), 256)
    mine = [r[:, lanes] for r in (master, one, two)]
    theirs = [given[rows(n, 32), :] for n in range(3)]
    results, copies = [], []
    for block in range(2):
        grad = jnp.concatenate(
            [total[block * 32 : block * 32 + 32], total[64 + block * 32 : 96 + block * 32]], axis=1
        )
        old, moment_one, moment_two = (
            jnp.where(c == block, a, b) for a, b in zip(mine, theirs)
        )
        moment_one = 0.9 * moment_one + 0.1 * grad
        moment_two = 0.95 * moment_two + 0.05 * grad * grad
        first_fix = 1.0 - 0.9**STEP
        second_fix = 1.0 - 0.95**STEP
        update = (
            moment_one / first_fix / (jnp.sqrt(moment_two / second_fix) + 1e-08) + 0.1 * old
        )
        weights = old - 0.002 * update
        results.append((weights, moment_one, moment_two))
        copies.append(weights.astype(BF16))
    for n in range(3):
        kept[rows(n, 32), :] = jnp.where(c == 0, results[0][n], results[1][n])
        sent[rows(n, 32), :] = jnp.where(c == 0, results[1][n], results[0][n])
    block = jnp.concatenate(
        [copies[0][:, 0:T], copies[1][:, 0:T], copies[0][:, T:], copies[1][:, T:]], axis=0
    )
    for n in range(8):
        out[rows(n), :] = block


def join_kernel(place, kept, given, *outs):
    first = place[2] == 0
    for n, out in enumerate(outs):
        a, b = kept[rows(n, 32), :], given[rows(n, 32), :]
        out[:, 0:256] = jnp.where(first, a, b)
        out[:, 256:512] = jnp.where(first, b, a)


def products(halves, tokens):
    totals = [None, None]
    for i in range(4 * len(halves)):
        parts = []
        for p in range(2):
            at = [((i % 4 * 4 + zh) * 2 + p) * 64 for zh in range(4)]
            parts.append(jnp.concatenate([halves[i // 4][a : a + 64, :] for a in at], axis=0))
        weight = jnp.concatenate(parts, axis=1)
        for n in range(2):
            part = jnp.dot(tokens(n, i), weight, preferred_element_type=F32)
            totals[n] = part if totals[n] is None else totals[n] + part
    return totals


def first_head_kernel(place, w0, w1, *refs):
    terms = products((w0, w1), lambda n, i: refs[n * 8 + i][...])
    for n, term in enumerate(terms):
        refs[16][rows(n, 256), :] = term


def next_head_kernel(place, w0, w1, *refs):
    before, total = refs[16:]
    terms = products((w0, w1), lambda n, i: refs[n * 8 + i][...])
    for n, term in enumerate(terms):
        total[rows(n, 256), :] = before[rows(n, 256), :] + term


def last_head_kernel(place, w0, w1, *refs):
    before, labels, labels_r, stats, stats_r = refs[2:]
    totals = products((w0, w1), lambda n, i: refs[n][:, rows(i, 256)])
    lane = lax.broadcasted_iota(I32, (256, T), 1)
    column = lax.broadcasted_iota(I32, (256, 256), 1) + place[2] * 256
    for n, (label, out) in enumerate(((labels, stats), (labels_r, stats_r))):
        logits = before[rows(n, 256), :] + totals[n]
        top = jnp.max(logits, axis=1, keepdims=True)
        expsum = jnp.sum(jnp.exp(logits - top), axis=1, keepdims=True)
        hit = jnp.sum(jnp.where(column == label[...], logits, 0.0), axis=1, keepdims=True)
        found = jnp.where(lane == 0, top, jnp.where(lane == 1, expsum, hit))
        out[...] = found.T[0:8, :]


def loss_kernel(place, a, b, out):
    a, b = a[...], b[...]
    top = jnp.maximum(a[0:1, :], b[0:1, :])
    total = a[1:2, :] * jnp.exp(a[0:1, :] - top) + b[1:2, :] * jnp.exp(b[0:1, :] - top)
    out[...] = top + jnp.log(total) - (a[2:3, :] + b[2:3, :])


def shape(*dims, dtype=F32):
    return jax.ShapeDtypeStruct(dims, dtype)


def whole(*dims):
    return pl.BlockSpec(dims, lambda *_: (0,) * len(dims))


def call(kernel, outs, place, args, specs=None, scratch=()):
    many = isinstance(outs, (list, tuple))
    specs = specs or [None] * len(args)
    specs = [s or whole(*a.shape) for s, a in zip(specs, args)]
    return pl.pallas_call(
        kernel,
        out_shape=outs,
        grid_spec=pltpu.PrefetchScalarGridSpec(
            num_scalar_prefetch=1,
            grid=(1,),
            in_specs=specs,
            out_specs=[whole(*o.shape) for o in outs] if many else whole(*outs.shape),
            scratch_shapes=scratch,
        ),
        compiler_params=pltpu.CompilerParams(vmem_limit_bytes=10 * 1024 * 1024),
        cost_estimate=pl.CostEstimate(flops=1, bytes_accessed=1, transcendentals=0),
    )(place, *args)


def columns(far, sign, other=False, nears=(0, 1, 2, 3)):
    def index(near, zl, place):
        x, y, c = place[0], place[1], place[2]
        c = 1 - c if other else c
        x = x + 8 + sign * (far * (1 - c) + near * c)
        y = y + 8 + sign * (far * c + near * (1 - c))
        return 0, lax.rem(x, 4) * 8 + zl * 4 + lax.rem(y, 4)

    return [
        pl.BlockSpec((256, 256), lambda _, p, near=near, zl=zl: index(near, zl, p))
        for near in nears
        for zl in range(2)
    ]


def swap(a):
    return lax.ppermute(a, "c", [(0, 1), (1, 0)])


def send(a, by, first):
    pairs = []
    for i in range(256):
        x, y, c = i // 64, i // 8 % 4, i % 2
        to = (x + by) % 4, (y + by) % 4
        pairs.append((i, i + ((to[0] - x) * 64 if (c == 0) == first else (to[1] - y) * 8)))
    return lax.ppermute(a, AXES, pairs)


def on_device(
    hidden_first, logit_grads, hidden_second, labels_second, master, moment_one, moment_two
):
    hold = lax.optimization_barrier
    place = jnp.stack([lax.axis_index(a) for a in ("x", "y", "c")])
    labels = labels_second[:, None]
    states = (master, moment_one, moment_two)
    far_half = (1 - place[2]) * 256
    state = jnp.concatenate([lax.dynamic_slice(a, (0, far_half), (32, 256)) for a in states])

    other_grads = swap(logit_grads)
    def pick(far, after):
        h, after = hold((hidden_first, after))
        args = [h] * 8
        block = shape(256, 2048, dtype=BF16)
        return call(pick_kernel, block, place, args, columns(far, 1, True)), after

    def grad(far, half, taken, *relayed):
        return call(
            grad_kernel,
            shape(2080, T, dtype=I16),
            place,
            (turned, *[hidden_first] * 4, taken, *relayed),
            [None]
            + columns(far, 1, nears=(2 * half, 2 * half + 1))
            + [pl.BlockSpec((256, 1024), lambda _, p: (0, half))]
            + [None] * len(relayed),
        )

    block, _ = pick(ORDER[0], place)
    block, other_grads = hold((block, other_grads))
    taken = swap(block)
    half = pl.BlockSpec((256, 256), lambda step, p: (0, p[2]))
    turned = call(
        turn_kernel,
        shape(256, 512, dtype=BF16),
        place,
        (logit_grads, other_grads),
        [half, half],
    )
    block, turned = pick(ORDER[1], turned)
    following = swap(block)
    relayed = send(grad(2, 0, taken), 1, True)
    last = grad(2, 1, taken)
    block, last = pick(3, last)
    other_relayed = send(last, 3, True)
    taken, following = following, swap(block)
    turned, block = hold((turned, block))
    last = grad(1, 1, taken)
    from_behind = [None, send(last, 1, True)]
    turned, last = hold((turned, last))
    last = grad(3, 0, following)
    block, last = pick(0, last)
    from_ahead = [send(last, 3, True), None]
    turned, block = hold((turned, block))
    from_behind[0] = send(grad(1, 0, taken, relayed), 1, True)
    from_ahead[1] = send(grad(3, 1, following, other_relayed), 3, True)
    taken = swap(block)
    own = [grad(0, 0, taken), grad(0, 1, taken)]
    sums = [own, from_behind, from_ahead]
    own[1], state = hold((own[1], state))
    state = swap(state)

    blocks = [None] * 4
    for far in ORDER + (0,):
        spec = pl.BlockSpec((1040, T), lambda s, p, far=far: (far % 2, 0))
        blocks[far] = call(
            sum_kernel,
            shape(1040, T, dtype=I16),
            place,
            [taken[far // 2] for taken in sums],
            [spec] * 3,
        )
        if far:
            blocks[far] = send(blocks[far], far, False)
    blocks[0], state = hold((blocks[0], state))
    chunks = call(second_sum_kernel, shape(1152, T, dtype=I16), place, blocks)
    chunks, second, labels = hold((chunks, hidden_second, labels))
    other_second, other_labels = swap(second), swap(labels)
    chunks = lax.all_to_all(chunks, ("zl", "zh"), 0, 0, tiled=True)
    kept, sent, copies = call(
        owner_kernel,
        [shape(96, 256)] * 2 + [shape(1024, T, dtype=BF16)],
        place,
        (chunks, *states, state),
    )
    copies = lax.all_to_all(copies, ("zl", "zh"), 0, 0, tiled=True)
    pieces = [copies] + [None] * 3
    for far in ORDER:
        pieces[far] = send(copies, far, False)
    picked = [
        call(pick_kernel, shape(256, 2048, dtype=BF16), place, [h] * 8, columns(2, -1))
        for h in (hidden_second, other_second)
    ]
    pieces, picked, other_labels = hold((pieces, picked, other_labels))
    own = jnp.concatenate(pieces[:2]), jnp.concatenate(pieces[2:])
    behind, ahead = [None, None], [None, None]
    behind[0], ahead[1] = send(own[0], 1, True), send(own[1], 3, True)
    behind[1], ahead[0] = send(own[1], 1, True), send(own[0], 3, True)
    def head(kernel, places, halves, *before):
        specs = [columns(far, -1, nears=(2 * half, 2 * half + 1)) for far, half in places]
        return call(
            kernel,
            shape(512, 256),
            place,
            (*halves, *[hidden_second] * 8, *[other_second] * 8, *before),
            [None] * 2 + (specs[0] + specs[1]) * 2 + [None] * len(before),
        )

    total = head(first_head_kernel, ((0, 0), (0, 1)), own)
    behind[0], ahead[1], total = hold((behind[0], ahead[1], total))
    two = send(behind[0], 1, True), send(ahead[1], 3, True)
    total = head(next_head_kernel, ((1, 0), (3, 1)), (behind[0], ahead[1]), total)
    behind[1], total, sent = hold((behind[1], total, sent))
    sent = swap(sent)
    total = head(next_head_kernel, ((1, 1), (3, 0)), (behind[1], ahead[0]), total)
    two, total, sent = hold((two, total, sent))
    stats, other_stats = call(
        last_head_kernel,
        [shape(8, 256)] * 2,
        place,
        (*two, *picked, total, labels, other_labels),
    )
    updated = call(join_kernel, [shape(32, 512)] * 3, place, (kept, sent))
    other_stats, updated = hold((swap(other_stats), updated))
    loss = call(loss_kernel, shape(1, 256), place, (stats, other_stats))
    return *updated, loss.reshape(256)


def solution(mesh):
    fine = Mesh(mesh.devices.reshape(SIZES), AXES)
    two, one = P(AXES, None), P(AXES)
    return jax.shard_map(
        on_device,
        mesh=fine,
        in_specs=(two, two, two, one, two, two, two),
        out_specs=(two, two, two, one),
        check_vma=False,
    )
```

```python
import jax
import jax.numpy as jnp
from jax import lax
from jax.experimental import pallas as pl
from jax.experimental.pallas import tpu as pltpu
from jax.sharding import Mesh
from jax.sharding import PartitionSpec as P

STEP = 10
AXES = ("x", "zl", "y", "zh", "c")
SIZES = (4, 2, 4, 4, 2)
F32, BF16, I16, I32 = jnp.float32, jnp.bfloat16, jnp.int16, jnp.int32
T = 128
ROUND = 12582912.0
ORDER = (2, 1, 3)


def encode(tiles):
    most = [jnp.max(jnp.abs(tile), axis=0, keepdims=True) for tile in tiles]
    most = jnp.concatenate(most, axis=0)
    level = jnp.floor(8.0 * (14.98 - jnp.log2(jnp.maximum(most, 1e-30))))
    scale = jnp.exp2(level * 0.125)
    whole_numbers = [
        ((tile * scale[i : i + 1, :] + ROUND) - ROUND).astype(I32).astype(I16)
        for i, tile in enumerate(tiles)
    ]
    return whole_numbers, level


def rows(i, n=T):
    return slice(i * n, (i + 1) * n)


def levels_tile(level):
    level = jnp.concatenate([level, jnp.zeros((16 - level.shape[0], T), F32)], axis=0)
    return level.astype(I32).astype(I16)


def scales_of(ref, first):
    level = ref[first : first + 16, :].astype(I32).astype(F32)
    return jnp.exp2(level * -0.125)


def added(refs, i, block=0):
    total = None
    for ref in refs:
        part = ref[block + i * 256 : block + i * 256 + 256, :].astype(I32).astype(F32)
        part *= scales_of(ref, block + 1024)[i : i + 1, :]
        total = part if total is None else total + part
    return total


def turn_kernel(place, l, lr, out):
    out[:, 0:256] = l[...].T
    out[:, 256:512] = lr[...].T


def pick_kernel(place, *refs):
    for i, h in enumerate(refs[:8]):
        refs[8][:, rows(i, 256)] = h[...]


def store(out, tiles):
    tiles, level = encode(tiles)
    for a in range(len(tiles) // 4):
        at = a * 1040
        for i in range(4):
            out[at + i * 256 : at + i * 256 + 256, :] = tiles[a * 4 + i]
        out[at + 1024 : at + 1040, :] = levels_tile(level[rows(a, 4), :])


def grad_kernel(place, lt, *refs):
    hr, relayed, out, tiles = refs[4], refs[5:-1], refs[-1], []
    for i, h in enumerate(refs[:4]):
        prod = jnp.dot(lt[:, 0:256], h[...], preferred_element_type=F32)
        prod += jnp.dot(lt[:, 256:512], hr[:, rows(i, 256)], preferred_element_type=F32)
        for half in range(2):
            tile = prod[:, rows(half)]
            if relayed:
                tile += added(relayed, i % 2 * 2 + half, i // 2 * 1040)
            tiles.append(tile)
    store(out, tiles)


def sum_kernel(place, *refs):
    store(refs[-1], [added(refs[:-1], i) for i in range(4)])


def second_sum_kernel(place, m0, m1, m2, m3, out):
    low = lax.broadcasted_iota(I32, (T, T), 1) < 64
    tiles = []
    for i in range(4):
        total = added((m0, m1, m2, m3), i)
        a, b = total[0:T, :], total[T:256, :]
        tiles.append(jnp.where(low, a, pltpu.roll(b, 64, 1)))
        tiles.append(jnp.where(low, pltpu.roll(a, 64, 1), b))
    tiles, level = encode(tiles)
    for i in range(8):
        out[i * 144 : i * 144 + T, :] = tiles[i]
        out[i * 144 + T : i * 144 + 144, :] = levels_tile(level[i : i + 1, :])


def owner_kernel(place, taken, master, one, two, given, kept, sent, out):
    c = place[2]
    total = None
    for n in range(8):
        at = n * 144
        inverse = scales_of(taken, at + T)[0:1, :]
        part = taken[at : at + T, :].astype(I32).astype(F32) * inverse
        total = part if total is None else total + part
    total = total.T
    lanes = pl.ds(pl.multiple_of(c * 256, 256), 256)
    mine = [r[:, lanes] for r in (master, one, two)]
    theirs = [given[rows(n, 32), :] for n in range(3)]
    results, copies = [], []
    for block in range(2):
        grad = jnp.concatenate(
            [total[block * 32 : block * 32 + 32], total[64 + block * 32 : 96 + block * 32]], axis=1
        )
        old, moment_one, moment_two = (
            jnp.where(c == block, a, b) for a, b in zip(mine, theirs)
        )
        moment_one = 0.9 * moment_one + 0.1 * grad
        moment_two = 0.95 * moment_two + 0.05 * grad * grad
        first_fix = 1.0 - 0.9**STEP
        second_fix = 1.0 - 0.95**STEP
        update = (
            moment_one / first_fix / (jnp.sqrt(moment_two / second_fix) + 1e-08) + 0.1 * old
        )
        weights = old - 0.002 * update
        results.append((weights, moment_one, moment_two))
        copies.append(weights.astype(BF16))
    for n in range(3):
        kept[rows(n, 32), :] = jnp.where(c == 0, results[0][n], results[1][n])
        sent[rows(n, 32), :] = jnp.where(c == 0, results[1][n], results[0][n])
    block = jnp.concatenate(
        [copies[0][:, 0:T], copies[1][:, 0:T], copies[0][:, T:], copies[1][:, T:]], axis=0
    )
    for n in range(8):
        out[rows(n), :] = block


def join_kernel(place, kept, given, *outs):
    first = place[2] == 0
    for n, out in enumerate(outs):
        a, b = kept[rows(n, 32), :], given[rows(n, 32), :]
        out[:, 0:256] = jnp.where(first, a, b)
        out[:, 256:512] = jnp.where(first, b, a)


def products(halves, tokens):
    totals = [None, None]
    for i in range(4 * len(halves)):
        parts = []
        for p in range(2):
            at = [((i % 4 * 4 + zh) * 2 + p) * 64 for zh in range(4)]
            parts.append(jnp.concatenate([halves[i // 4][a : a + 64, :] for a in at], axis=0))
        weight = jnp.concatenate(parts, axis=1)
        for n in range(2):
            part = jnp.dot(tokens(n, i), weight, preferred_element_type=F32)
            totals[n] = part if totals[n] is None else totals[n] + part
    return totals


def first_head_kernel(place, w0, w1, *refs):
    terms = products((w0, w1), lambda n, i: refs[n * 8 + i][...])
    for n, term in enumerate(terms):
        refs[16][rows(n, 256), :] = term


def next_head_kernel(place, w0, w1, *refs):
    before, total = refs[16:]
    terms = products((w0, w1), lambda n, i: refs[n * 8 + i][...])
    for n, term in enumerate(terms):
        total[rows(n, 256), :] = before[rows(n, 256), :] + term


def last_head_kernel(place, w0, w1, *refs):
    before, labels, labels_r, stats, stats_r = refs[2:]
    totals = products((w0, w1), lambda n, i: refs[n][:, rows(i, 256)])
    lane = lax.broadcasted_iota(I32, (256, T), 1)
    column = lax.broadcasted_iota(I32, (256, 256), 1) + place[2] * 256
    for n, (label, out) in enumerate(((labels, stats), (labels_r, stats_r))):
        logits = before[rows(n, 256), :] + totals[n]
        top = jnp.max(logits, axis=1, keepdims=True)
        expsum = jnp.sum(jnp.exp(logits - top), axis=1, keepdims=True)
        hit = jnp.sum(jnp.where(column == label[...], logits, 0.0), axis=1, keepdims=True)
        found = jnp.where(lane == 0, top, jnp.where(lane == 1, expsum, hit))
        out[...] = found.T[0:8, :]


def loss_kernel(place, a, b, out):
    a, b = a[...], b[...]
    top = jnp.maximum(a[0:1, :], b[0:1, :])
    total = a[1:2, :] * jnp.exp(a[0:1, :] - top) + b[1:2, :] * jnp.exp(b[0:1, :] - top)
    out[...] = top + jnp.log(total) - (a[2:3, :] + b[2:3, :])


def shape(*dims, dtype=F32):
    return jax.ShapeDtypeStruct(dims, dtype)


def whole(*dims):
    return pl.BlockSpec(dims, lambda *_: (0,) * len(dims))


def call(kernel, outs, place, args, specs=None, vmem=6):
    many = isinstance(outs, (list, tuple))
    specs = specs or [None] * len(args)
    specs = [s or whole(*a.shape) for s, a in zip(specs, args)]
    return pl.pallas_call(
        kernel,
        out_shape=outs,
        grid_spec=pltpu.PrefetchScalarGridSpec(
            num_scalar_prefetch=1,
            grid=(1,),
            in_specs=specs,
            out_specs=[whole(*o.shape) for o in outs] if many else whole(*outs.shape),
        ),
        compiler_params=pltpu.CompilerParams(vmem_limit_bytes=vmem * 1024 * 1024),
        cost_estimate=pl.CostEstimate(flops=1, bytes_accessed=1, transcendentals=0),
    )(place, *args)


def columns(far, sign, other=False, nears=(0, 1, 2, 3)):
    def index(near, zl, place):
        x, y, c = place[0], place[1], place[2]
        c = 1 - c if other else c
        x = x + 8 + sign * (far * (1 - c) + near * c)
        y = y + 8 + sign * (far * c + near * (1 - c))
        return 0, lax.rem(x, 4) * 8 + zl * 4 + lax.rem(y, 4)

    return [
        pl.BlockSpec((256, 256), lambda _, p, near=near, zl=zl: index(near, zl, p))
        for near in nears
        for zl in range(2)
    ]


def swap(a):
    return lax.ppermute(a, "c", [(0, 1), (1, 0)])


def send(a, by, first):
    pairs = []
    for i in range(256):
        x, y, c = i // 64, i // 8 % 4, i % 2
        to = (x + by) % 4, (y + by) % 4
        pairs.append((i, i + ((to[0] - x) * 64 if (c == 0) == first else (to[1] - y) * 8)))
    return lax.ppermute(a, AXES, pairs)


def on_device(
    hidden_first, logit_grads, hidden_second, labels_second, master, moment_one, moment_two
):
    hold = lax.optimization_barrier
    place = jnp.stack([lax.axis_index(a) for a in ("x", "y", "c")])
    labels = labels_second[:, None]
    states = (master, moment_one, moment_two)
    far_half = (1 - place[2]) * 256
    state = jnp.concatenate([lax.dynamic_slice(a, (0, far_half), (32, 256)) for a in states])

    other_grads = swap(logit_grads)
    def pick(far, after):
        h, after = hold((hidden_first, after))
        args = [h] * 8
        block = shape(256, 2048, dtype=BF16)
        return call(pick_kernel, block, place, args, columns(far, 1, True, (0, 2, 1, 3))), after

    def grad(far, half, taken, *relayed):
        return call(
            grad_kernel,
            shape(2080, T, dtype=I16),
            place,
            (turned, *[hidden_first] * 4, taken, *relayed),
            [None]
            + columns(far, 1, nears=(half, half + 2))
            + [pl.BlockSpec((256, 1024), lambda _, p: (0, half))]
            + [None] * len(relayed),
        )

    block, _ = pick(ORDER[0], place)
    block, other_grads = hold((block, other_grads))
    taken = swap(block)
    half = pl.BlockSpec((256, 256), lambda step, p: (0, p[2]))
    turned = call(
        turn_kernel,
        shape(256, 512, dtype=BF16),
        place,
        (logit_grads, other_grads),
        [half, half],
    )
    block, turned = pick(ORDER[1], turned)
    following = swap(block)
    relayed = send(grad(2, 0, taken), 1, True)
    last = grad(2, 1, taken)
    block, last = pick(3, last)
    other_relayed = send(last, 3, True)
    taken, following = following, swap(block)
    turned, block = hold((turned, block))
    last = grad(1, 1, taken)
    from_behind = [None, send(last, 1, True)]
    turned, last = hold((turned, last))
    last = grad(3, 0, following)
    block, last = pick(0, last)
    from_ahead = [send(last, 3, True), None]
    turned, block = hold((turned, block))
    from_behind[0] = send(grad(1, 0, taken, relayed), 1, True)
    from_ahead[1] = send(grad(3, 1, following, other_relayed), 3, True)
    taken = swap(block)
    own = [grad(0, 0, taken), grad(0, 1, taken)]
    sums = [own, from_behind, from_ahead]
    own[1], state = hold((own[1], state))
    state = swap(state)

    blocks = [None] * 4
    for far in ORDER + (0,):
        spec = pl.BlockSpec((1040, T), lambda s, p, far=far: (far // 2, 0))
        blocks[far] = call(
            sum_kernel,
            shape(1040, T, dtype=I16),
            place,
            [taken[far % 2] for taken in sums],
            [spec] * 3,
        )
        if far:
            blocks[far] = send(blocks[far], far, False)
    blocks[0], state = hold((blocks[0], state))
    chunks = call(second_sum_kernel, shape(1152, T, dtype=I16), place, blocks)
    chunks = lax.all_to_all(chunks, ("zl", "zh"), 0, 0, tiled=True)
    chunks, second, labels = hold((chunks, hidden_second, labels))
    other_second, other_labels = swap(second), swap(labels)
    kept, sent, copies = call(
        owner_kernel,
        [shape(96, 256)] * 2 + [shape(1024, T, dtype=BF16)],
        place,
        (chunks, *states, state),
    )
    copies = lax.all_to_all(copies, ("zl", "zh"), 0, 0, tiled=True)
    pieces = [copies] + [None] * 3
    for far in ORDER:
        pieces[far] = send(copies, far, False)
    picked = [
        call(pick_kernel, shape(256, 2048, dtype=BF16), place, [h] * 8, columns(2, -1))
        for h in (hidden_second, other_second)
    ]
    pieces, picked, other_labels = hold((pieces, picked, other_labels))
    own = jnp.concatenate(pieces[:2]), jnp.concatenate(pieces[2:])
    behind, ahead = [None, None], [None, None]
    behind[0], ahead[1] = send(own[0], 1, True), send(own[1], 3, True)
    behind[1], ahead[0] = send(own[1], 1, True), send(own[0], 3, True)
    def head(kernel, places, halves, *before):
        specs = [columns(far, -1, nears=(2 * half, 2 * half + 1)) for far, half in places]
        return call(
            kernel,
            shape(512, 256),
            place,
            (*halves, *[hidden_second] * 8, *[other_second] * 8, *before),
            [None] * 2 + (specs[0] + specs[1]) * 2 + [None] * len(before),
            10,
        )

    total = head(first_head_kernel, ((0, 0), (0, 1)), own)
    behind[0], ahead[1], total = hold((behind[0], ahead[1], total))
    two = send(behind[0], 1, True), send(ahead[1], 3, True)
    total = head(next_head_kernel, ((1, 0), (3, 1)), (behind[0], ahead[1]), total)
    behind[1], total, sent = hold((behind[1], total, sent))
    sent = swap(sent)
    total = head(next_head_kernel, ((1, 1), (3, 0)), (behind[1], ahead[0]), total)
    two, total, sent = hold((two, total, sent))
    stats, other_stats = call(
        last_head_kernel,
        [shape(8, 256)] * 2,
        place,
        (*two, *picked, total, labels, other_labels),
        None,
        10,
    )
    updated = call(join_kernel, [shape(32, 512)] * 3, place, (kept, sent))
    other_stats, updated = hold((swap(other_stats), updated))
    loss = call(loss_kernel, shape(1, 256), place, (stats, other_stats))
    return *updated, loss.reshape(256)


def solution(mesh):
    fine = Mesh(mesh.devices.reshape(SIZES), AXES)
    two, one = P(AXES, None), P(AXES)
    return jax.shard_map(
        on_device,
        mesh=fine,
        in_specs=(two, two, two, one, two, two, two),
        out_specs=(two, two, two, one),
        check_vma=False,
    )
```
